32 devices in a mesh: chan: 8 (over z, y), tm: 4 (over x, core).
Axes of the slice: x: 2, y: 2, z: 4, core: 2. Of those that a mesh axis runs over, the one named last changes fastest.
Arguments:
- record: float32 [64, 256, 16384], P('tm', 'chan'), may hold values from -6 to 6
- fir_taps: float32 [64], replicated, may hold values from -0.75 to 0.75
- pair_offsets: int32 [8], replicated, may hold values from -128 to 128, as said below
Outputs:
- correlation: float32 [8, 256, 16384], P('tm', None, 'chan')
The draws below stay inside these ranges and needn't reach their ends.
Inputs may be any that keep to these rules, and one draw needn't show every extreme that they name: `pair_offsets`: 8 distinct nonzero channel offsets; both -128 and 128 are among them.
All inputs are finite; a program needn't handle non-finite values.
Results may differ from the reference program's by a relative error of at most 0.000098.
Values sent between devices are 32-bit elements; how exact they have to be, the bound alone decides.
A program may use at most 320 MiB of HBM per device.

```python
import math
import jax
import jax.numpy as jnp
from jax import lax

C = 16384
S = 256
TAPS = 64
R = 128
K = 8
SEGS = 64
HALF = 128


def draw_pair_offsets(key, part):
    shuffled = jax.random.permutation(key, 2 * R - 2)
    interior = shuffled[:K - 2] + 1
    interior = jnp.where(interior <= R - 1, interior, R - 1 - interior)
    extremes = jnp.array([-R, R], dtype=jnp.int32)
    merged = jnp.concatenate([extremes, interior.astype(jnp.int32)])
    return jax.random.permutation(jax.random.fold_in(key, 7), merged)


def levels(key, dims, shards, smallest, largest):
    loudness, own = 1.0, jax.random.fold_in(key, 6)
    for position, blocks in shards:
        steps = jnp.exp(jax.random.uniform(jax.random.fold_in(own, position), (blocks,), jnp.float32, smallest / len(shards), largest / len(shards)))
        loudness = loudness * jnp.repeat(steps, dims[position] // blocks).reshape([-1 if axis == position else 1 for axis in range(len(dims))])
    return loudness


def noise(key, shape, scale, limit, pieces=(), held_as=jnp.bfloat16):
    result = scale * jax.random.normal(key, shape, jnp.float32)
    if pieces:
        result = result * levels(key, shape, pieces, -0.22, 0.18)
    return jnp.clip(result, -limit, limit).astype(held_as)


def setup_inputs(seed: int = 0) -> dict:
    streams_of = jax.random.split(jax.random.key(seed), 4)
    return {
        "record": noise(streams_of[0], (SEGS, S, C), 1.0, 6.0, ((0, 4), (1, 8)), jnp.float32),
        "fir_taps": noise(streams_of[1], (TAPS,), TAPS ** -0.5, 0.75, (), jnp.float32),
        "pair_offsets": draw_pair_offsets(jax.random.fold_in(streams_of[3], 71), 0),
    }


def reference(record, fir_taps, pair_offsets):
    length = 2 * S
    tap_spec = jnp.fft.rfft(fir_taps, n=length)
    raw_spec = jnp.fft.rfft(record, n=length, axis=1)
    whitened = jnp.fft.irfft(raw_spec * tap_spec[None, :, None], n=length, axis=1)[:, :S, :]
    spectra = jnp.fft.rfft(whitened, n=length, axis=1)
    norm_scale = 1.0 / math.sqrt(SEGS * S)

    def one_offset(offset):
        partner = jnp.roll(spectra, -offset, axis=2)
        cross_spec = lax.optimization_barrier(jnp.sum(jnp.conj(spectra) * partner, axis=0))
        circular = jnp.fft.irfft(cross_spec, n=length, axis=0)
        return jnp.concatenate([circular[length - HALF:], circular[:HALF]], axis=0) * norm_scale
    return lax.map(one_offset, pair_offsets).astype(jnp.float32)
```

```python
import functools
import math

import jax
import jax.numpy as jnp
import numpy as np
from jax import lax
from jax.experimental import pallas as pl
from jax.experimental.pallas import tpu as pltpu
from jax.sharding import PartitionSpec as P

R = 128
WIDE = 2 * R
AHEAD = 3
SLOTS = 4
ROWS = 64
LANES = 128
F32, BF16 = jnp.float32, jnp.bfloat16


def tables(seg_len, norm_scale):
    period = 2 * seg_len
    odd = 2 * np.arange(seg_len) + 1
    turn = 2.0 * math.pi / (2 * period)
    forward = np.outer(np.arange(seg_len), odd) % (2 * period) * turn
    inverse = np.outer(np.arange(seg_len) - seg_len // 2, odd) % (2 * period) * turn
    forward = np.concatenate([np.cos(forward), np.sin(forward)], axis=1)
    inverse = np.concatenate([np.cos(inverse), np.sin(inverse)], axis=1)
    return (
        forward.astype(np.float32),
        (inverse * (2.0 / period * norm_scale)).astype(np.float32),
    )


def halves(value):
    high = value.astype(BF16)
    return high, (value - high.astype(F32)).astype(BF16)


def product(left, right, dims):
    dot = lambda a, b: lax.dot_general(a, b, (dims, ((), ())), preferred_element_type=F32)
    return dot(left[0], right[0]) + (dot(left[0], right[1]) + dot(left[1], right[0]))


def kernel(
    n_chan, n_time, record, taps, offsets, forward, inv_high, inv_low, out, landed,
    spec, acc, part, inbox, xbuf, mat_high, mat_low,
    send_sem, recv_sem, load_sem, part_sem, inbox_sem,
):
    me, mine = lax.axis_index("chan"), lax.axis_index("tm")
    segs, rows, channels = record.shape
    seg_len = rows * n_chan
    block = channels // n_chan
    pieces = block // WIDE + 1
    per_time = part.shape[1] // n_time

    barrier = pltpu.get_barrier_semaphore()

    def greet_chan(r, _):
        pl.semaphore_signal(
            barrier, inc=1, device_id={"chan": lax.rem(me + r, n_chan)},
            device_id_type=pl.DeviceIdType.MESH,
        )
        return 0

    def greet_time(r, _):
        pl.semaphore_signal(
            barrier, inc=1, device_id={"tm": lax.rem(mine + r, n_time)},
            device_id_type=pl.DeviceIdType.MESH,
        )
        return 0

    lax.fori_loop(1, n_chan, greet_chan, 0)
    lax.fori_loop(1, n_time, greet_time, 0)
    pl.semaphore_wait(barrier, n_chan + n_time - 2)

    def place(piece, half, width):
        columns = pl.ds(half * R, width)
        return landed.at[piece, :, pl.ds(pl.multiple_of(me * rows, 8), rows), columns]

    def source(owner, piece, half, width):
        first = lax.rem(owner * block + piece * WIDE + half * R + (channels - R), channels)
        return record.at[:, :, pl.ds(pl.multiple_of(first, R), width)]

    def send(piece, cuts):
        for half, width in cuts:
            pltpu.make_async_copy(
                source(me, piece, half, width), place(piece, half, width), recv_sem.at[piece]
            ).start()

        def to(r, _):
            owner = lax.rem(me + r, n_chan)
            for half, width in cuts:
                pltpu.make_async_remote_copy(
                    src_ref=source(owner, piece, half, width),
                    dst_ref=place(piece, half, width),
                    send_sem=send_sem.at[piece],
                    recv_sem=recv_sem.at[piece],
                    device_id={"chan": owner},
                    device_id_type=pl.DeviceIdType.MESH,
                ).start()
            return 0

        lax.fori_loop(1, n_chan, to, 0)

    def send_any(piece):
        edge = (piece == 0) | (piece == pieces - 1)

        @pl.when(edge)
        def _():
            send(piece, ((0, R), (1, R)))

        @pl.when(jnp.logical_not(edge))
        def _():
            send(piece, ((0, WIDE),))

    for piece in range(min(AHEAD, pieces)):
        send(piece, ((0, R), (1, R)) if piece in (0, pieces - 1) else ((0, WIDE),))

    row_ids = lax.broadcasted_iota(jnp.int32, (seg_len, seg_len), 0)
    spread = lax.broadcasted_iota(jnp.int32, (seg_len, seg_len), 1) - row_ids
    acc[0, :, pl.ds(0, seg_len)] = jnp.zeros((seg_len, seg_len), F32)

    def add_tap(tap, _):
        acc[0, :, pl.ds(0, seg_len)] += jnp.where(spread == tap, taps[tap], 0.0)
        return 0

    lax.fori_loop(0, taps.shape[0], add_tap, 0)
    matrix = jnp.dot(
        acc[0, :, pl.ds(0, seg_len)], forward[...],
        precision=lax.Precision.HIGHEST, preferred_element_type=F32,
    )
    high, low = halves(matrix)
    mat_high[...] = high
    mat_low[...] = low

    def load(piece, seg):
        slot = lax.rem(seg, SLOTS)
        return pltpu.make_async_copy(landed.at[piece, seg], xbuf.at[slot], load_sem.at[slot])

    def transform(piece):
        for seg in range(SLOTS - 1):
            load(piece, seg).start()

        def one(seg, _):
            @pl.when(seg + (SLOTS - 1) < segs)
            def _():
                load(piece, seg + (SLOTS - 1)).start()

            load(piece, seg).wait()
            spec[seg, :, pl.ds(0, WIDE), :] = spec[seg, :, pl.ds(WIDE, WIDE), :]
            sample = halves(xbuf[lax.rem(seg, SLOTS)].T)
            for side in range(2):
                columns = pl.ds(side * seg_len, seg_len)
                found = product(
                    sample, (mat_high[:, columns], mat_low[:, columns]), (((1,), (0,)))
                )
                for lane in range(seg_len // LANES):
                    spec[seg, side * (seg_len // LANES) + lane, pl.ds(WIDE, WIDE), :] = found[
                        :, lane * LANES : (lane + 1) * LANES
                    ]
            return 0

        lax.fori_loop(0, segs, one, 0)

    lanes = seg_len // LANES

    def correlate(slot):
        def one_offset(k, _):
            offset = offsets[k]

            def rows_at(g, _):
                base = pl.multiple_of(g * ROWS, ROWS)
                for lane in range(lanes):
                    even = jnp.zeros((ROWS, LANES), F32)
                    odd = jnp.zeros((ROWS, LANES), F32)
                    for seg in range(segs):
                        own = pl.ds(base + R, ROWS)
                        other = pl.ds(base + R + offset, ROWS)
                        c, s = spec[seg, lane, own, :], spec[seg, lane + lanes, own, :]
                        c2, s2 = spec[seg, lane, other, :], spec[seg, lane + lanes, other, :]
                        even += c * c2 + s * s2
                        odd += c * s2 - s * c2
                    acc[k, pl.ds(base, ROWS), pl.ds(lane * LANES, LANES)] = even
                    acc[k, pl.ds(base, ROWS), pl.ds(seg_len + lane * LANES, LANES)] = odd
                return 0

            lax.fori_loop(0, WIDE // ROWS, rows_at, 0)
            part[slot, k] = product(
                (inv_high[...], inv_low[...]), halves(acc[k]), (((1,), (1,)))
            )
            return 0

        lax.fori_loop(0, part.shape[1], one_offset, 0)

    def share(i, slot):
        def to(r, _):
            peer = lax.rem(mine + r, n_time)
            pltpu.make_async_remote_copy(
                src_ref=part.at[slot, pl.ds(peer * per_time, per_time)],
                dst_ref=inbox.at[i, r - 1],
                send_sem=part_sem.at[slot],
                recv_sem=inbox_sem.at[i],
                device_id={"tm": peer},
                device_id_type=pl.DeviceIdType.MESH,
            ).start()
            return 0

        lax.fori_loop(1, n_time, to, 0)

    def wait_for(ref, sem):
        pltpu.make_async_copy(ref, ref, sem).wait()

    def finish(i):
        wait_for(inbox.at[i], inbox_sem.at[i])
        slot = lax.rem(i, 2)
        columns = pl.ds(pl.multiple_of(i * WIDE, WIDE), WIDE)
        for k in range(per_time):
            total = part[slot, mine * per_time + k]
            for r in range(n_time - 1):
                total += inbox[i, r, k]
            out[k, :, columns] = total

    def step(piece, _):
        wait_for(landed.at[piece], recv_sem.at[piece])

        @pl.when(piece + AHEAD < pieces)
        def _():
            send_any(piece + AHEAD)

        transform(piece)

        @pl.when(piece >= 1)
        def _():
            i = piece - 1
            slot = lax.rem(i, 2)

            @pl.when(i >= 2)
            def _():
                wait_for(inbox.at[i], part_sem.at[slot])

            correlate(slot)
            share(i, slot)

            @pl.when(i >= 1)
            def _():
                finish(i - 1)

        return 0

    lax.fori_loop(0, pieces, step, 0)
    finish(pieces - 2)
    for slot in range(min(2, pieces - 1)):
        wait_for(inbox.at[0], part_sem.at[slot])

    def drain(piece, _):
        wait_for(landed.at[piece, :, pl.ds(0, seg_len - rows)], send_sem.at[piece])
        return 0

    lax.fori_loop(0, pieces, drain, 0)


def per_device(record, fir_taps, pair_offsets):
    n_chan, n_time = lax.axis_size("chan"), lax.axis_size("tm")
    segs, rows, channels = record.shape
    seg_len, block, pairs = rows * n_chan, channels // n_chan, pair_offsets.shape[0]
    pieces = block // WIDE + 1
    forward, inverse = tables(seg_len, 1.0 / math.sqrt(segs * n_time * seg_len))
    inv_high = inverse.astype(jnp.bfloat16)
    inv_low = (inverse - inv_high.astype(np.float32)).astype(jnp.bfloat16)
    lanes = 2 * seg_len // LANES
    vmem, smem = pl.BlockSpec(memory_space=pltpu.VMEM), pl.BlockSpec(memory_space=pltpu.SMEM)
    anywhere = pl.BlockSpec(memory_space=pl.ANY)
    result, _ = pl.pallas_call(
        functools.partial(kernel, n_chan, n_time),
        out_shape=(
            jax.ShapeDtypeStruct((pairs // n_time, seg_len, block), F32),
            jax.ShapeDtypeStruct((pieces, segs, seg_len, WIDE), F32),
        ),
        in_specs=[anywhere, smem, smem, vmem, vmem, vmem],
        out_specs=(vmem, anywhere),
        scratch_shapes=[
            pltpu.VMEM((segs, lanes, 2 * WIDE, LANES), F32),
            pltpu.VMEM((pairs, WIDE, 2 * seg_len), F32),
            pltpu.VMEM((2, pairs, seg_len, WIDE), F32),
            pltpu.VMEM((pieces - 1, n_time - 1, pairs // n_time, seg_len, WIDE), F32),
            pltpu.VMEM((SLOTS, seg_len, WIDE), F32),
            pltpu.VMEM((seg_len, 2 * seg_len), BF16),
            pltpu.VMEM((seg_len, 2 * seg_len), BF16),
            pltpu.SemaphoreType.DMA((pieces,)),
            pltpu.SemaphoreType.DMA((pieces,)),
            pltpu.SemaphoreType.DMA((SLOTS,)),
            pltpu.SemaphoreType.DMA((2,)),
            pltpu.SemaphoreType.DMA((pieces - 1,)),
        ],
        compiler_params=pltpu.CompilerParams(
            collective_id=0, has_side_effects=True, vmem_limit_bytes=60 * 2**20
        ),
    )(record, fir_taps, pair_offsets, forward, inv_high, inv_low)
    return result


def solution(mesh):
    placed = (P("tm", "chan", None), P(), P())
    return jax.shard_map(
        per_device, mesh=mesh, in_specs=placed, out_specs=P("tm", None, "chan"), check_vma=False
    )
```

```python
import functools
import math

import jax
import jax.numpy as jnp
import numpy as np
from jax import lax
from jax.experimental import pallas as pl
from jax.experimental.pallas import tpu as pltpu
from jax.sharding import PartitionSpec as P

R = 128
WIDE = 2 * R
AHEAD = 3
SLOTS = 4
ROWS = 64
LANES = 128
F32, BF16 = jnp.float32, jnp.bfloat16


def tables(seg_len, norm_scale):
    period = 2 * seg_len
    odd = 2 * np.arange(seg_len) + 1
    turn = 2.0 * math.pi / (2 * period)
    forward = np.outer(np.arange(seg_len), odd) % (2 * period) * turn
    inverse = np.outer(np.arange(seg_len) - seg_len // 2, odd) % (2 * period) * turn
    forward = np.concatenate([np.cos(forward), np.sin(forward)], axis=1)
    inverse = np.concatenate([np.cos(inverse), np.sin(inverse)], axis=1)
    return (
        forward.astype(np.float32),
        (inverse * (2.0 / period * norm_scale)).astype(np.float32),
    )


def halves(value):
    high = value.astype(BF16)
    return high, (value - high.astype(F32)).astype(BF16)


def product(left, right, dims):
    dot = lambda a, b: lax.dot_general(a, b, (dims, ((), ())), preferred_element_type=F32)
    return dot(left[0], right[0]) + (dot(left[0], right[1]) + dot(left[1], right[0]))


def kernel(
    n_chan, n_time, record, taps, offsets, forward, inv_high, inv_low, out, landed,
    spec, acc, part, inbox, xbuf, mat_high, mat_low,
    send_sem, recv_sem, load_sem, part_sem, inbox_sem,
):
    me, mine = lax.axis_index("chan"), lax.axis_index("tm")
    segs, rows, channels = record.shape
    seg_len = rows * n_chan
    block = channels // n_chan
    pieces = block // WIDE + 1
    per_time = part.shape[1] // n_time

    barrier = pltpu.get_barrier_semaphore()

    def greet_chan(r, _):
        pl.semaphore_signal(
            barrier, inc=1, device_id={"chan": lax.rem(me + r, n_chan)},
            device_id_type=pl.DeviceIdType.MESH,
        )
        return 0

    def greet_time(r, _):
        pl.semaphore_signal(
            barrier, inc=1, device_id={"tm": lax.rem(mine + r, n_time)},
            device_id_type=pl.DeviceIdType.MESH,
        )
        return 0

    lax.fori_loop(1, n_chan, greet_chan, 0)
    lax.fori_loop(1, n_time, greet_time, 0)
    pl.semaphore_wait(barrier, n_chan + n_time - 2)

    def place(piece, half, width):
        columns = pl.ds(half * R, width)
        return landed.at[piece, :, pl.ds(pl.multiple_of(me * rows, 8), rows), columns]

    def source(owner, piece, half, width):
        first = lax.rem(owner * block + piece * WIDE + half * R + (channels - R), channels)
        return record.at[:, :, pl.ds(pl.multiple_of(first, R), width)]

    def send(piece, cuts):
        for half, width in cuts:
            pltpu.make_async_copy(
                source(me, piece, half, width), place(piece, half, width), recv_sem.at[piece]
            ).start()

        def to(r, _):
            owner = lax.rem(me + r, n_chan)
            for half, width in cuts:
                pltpu.make_async_remote_copy(
                    src_ref=source(owner, piece, half, width),
                    dst_ref=place(piece, half, width),
                    send_sem=send_sem.at[piece],
                    recv_sem=recv_sem.at[piece],
                    device_id={"chan": owner},
                    device_id_type=pl.DeviceIdType.MESH,
                ).start()
            return 0

        lax.fori_loop(1, n_chan, to, 0)

    def send_any(piece):
        edge = piece == pieces - 1

        @pl.when(edge)
        def _():
            send(piece, ((0, R),))

        @pl.when(jnp.logical_not(edge))
        def _():
            send(piece, ((0, WIDE),))

    for piece in range(min(AHEAD, pieces)):
        first, last = piece == 0, piece == pieces - 1
        send(piece, ((0, R), (1, R)) if first else ((0, R),) if last else ((0, WIDE),))

    edge_copy = pltpu.make_async_remote_copy(
        src_ref=landed.at[0, :, :, pl.ds(R, R)],
        dst_ref=landed.at[pieces - 1, :, :, pl.ds(R, R)],
        send_sem=send_sem.at[pieces],
        recv_sem=recv_sem.at[pieces - 1],
        device_id={"chan": lax.rem(me + n_chan - 1, n_chan)},
        device_id_type=pl.DeviceIdType.MESH,
    )

    row_ids = lax.broadcasted_iota(jnp.int32, (seg_len, seg_len), 0)
    spread = lax.broadcasted_iota(jnp.int32, (seg_len, seg_len), 1) - row_ids
    acc[0, :, pl.ds(0, seg_len)] = jnp.zeros((seg_len, seg_len), F32)

    def add_tap(tap, _):
        acc[0, :, pl.ds(0, seg_len)] += jnp.where(spread == tap, taps[tap], 0.0)
        return 0

    lax.fori_loop(0, taps.shape[0], add_tap, 0)
    matrix = jnp.dot(
        acc[0, :, pl.ds(0, seg_len)], forward[...],
        precision=lax.Precision.HIGHEST, preferred_element_type=F32,
    )
    high, low = halves(matrix)
    mat_high[...] = high
    mat_low[...] = low

    def load(piece, seg):
        slot = lax.rem(seg, SLOTS)
        return pltpu.make_async_copy(landed.at[piece, seg], xbuf.at[slot], load_sem.at[slot])

    def transform(piece):
        for seg in range(SLOTS - 1):
            load(piece, seg).start()

        def one(seg, _):
            @pl.when(seg + (SLOTS - 1) < segs)
            def _():
                load(piece, seg + (SLOTS - 1)).start()

            load(piece, seg).wait()
            spec[seg, :, pl.ds(0, WIDE), :] = spec[seg, :, pl.ds(WIDE, WIDE), :]
            sample = halves(xbuf[lax.rem(seg, SLOTS)].T)
            for side in range(2):
                columns = pl.ds(side * seg_len, seg_len)
                found = product(
                    sample, (mat_high[:, columns], mat_low[:, columns]), (((1,), (0,)))
                )
                for lane in range(seg_len // LANES):
                    spec[seg, side * (seg_len // LANES) + lane, pl.ds(WIDE, WIDE), :] = found[
                        :, lane * LANES : (lane + 1) * LANES
                    ]
            return 0

        lax.fori_loop(0, segs, one, 0)

    lanes = seg_len // LANES

    def correlate(slot):
        def one_offset(k, _):
            offset = offsets[k]

            def rows_at(g, _):
                base = pl.multiple_of(g * ROWS, ROWS)
                for lane in range(lanes):
                    even = jnp.zeros((ROWS, LANES), F32)
                    odd = jnp.zeros((ROWS, LANES), F32)
                    for seg in range(segs):
                        own = pl.ds(base + R, ROWS)
                        other = pl.ds(base + R + offset, ROWS)
                        c, s = spec[seg, lane, own, :], spec[seg, lane + lanes, own, :]
                        c2, s2 = spec[seg, lane, other, :], spec[seg, lane + lanes, other, :]
                        even += c * c2 + s * s2
                        odd += c * s2 - s * c2
                    acc[k, pl.ds(base, ROWS), pl.ds(lane * LANES, LANES)] = even
                    acc[k, pl.ds(base, ROWS), pl.ds(seg_len + lane * LANES, LANES)] = odd
                return 0

            lax.fori_loop(0, WIDE // ROWS, rows_at, 0)
            part[slot, k] = product(
                (inv_high[...], inv_low[...]), halves(acc[k]), (((1,), (1,)))
            )
            return 0

        lax.fori_loop(0, part.shape[1], one_offset, 0)

    def share(i, slot):
        def to(r, _):
            peer = lax.rem(mine + r, n_time)
            pltpu.make_async_remote_copy(
                src_ref=part.at[slot, pl.ds(peer * per_time, per_time)],
                dst_ref=inbox.at[i, r - 1],
                send_sem=part_sem.at[slot],
                recv_sem=inbox_sem.at[i],
                device_id={"tm": peer},
                device_id_type=pl.DeviceIdType.MESH,
            ).start()
            return 0

        lax.fori_loop(1, n_time, to, 0)

    def wait_for(ref, sem):
        pltpu.make_async_copy(ref, ref, sem).wait()

    def finish(i):
        wait_for(inbox.at[i], inbox_sem.at[i])
        slot = lax.rem(i, 2)
        columns = pl.ds(pl.multiple_of(i * WIDE, WIDE), WIDE)
        for k in range(per_time):
            total = part[slot, mine * per_time + k]
            for r in range(n_time - 1):
                total += inbox[i, r, k]
            out[k, :, columns] = total

    def step(piece, _):
        wait_for(landed.at[piece], recv_sem.at[piece])

        @pl.when(piece == 0)
        def _():
            edge_copy.start()

        @pl.when(piece + AHEAD < pieces)
        def _():
            send_any(piece + AHEAD)

        transform(piece)

        @pl.when(piece >= 1)
        def _():
            i = piece - 1
            slot = lax.rem(i, 2)

            @pl.when(i >= 2)
            def _():
                wait_for(inbox.at[i], part_sem.at[slot])

            correlate(slot)
            share(i, slot)

            @pl.when(i >= 1)
            def _():
                finish(i - 1)

        return 0

    lax.fori_loop(0, pieces, step, 0)
    finish(pieces - 2)
    for slot in range(min(2, pieces - 1)):
        wait_for(inbox.at[0], part_sem.at[slot])

    def drain(piece, _):
        wait_for(landed.at[piece, :, pl.ds(0, seg_len - rows)], send_sem.at[piece])
        return 0

    lax.fori_loop(0, pieces - 1, drain, 0)
    wait_for(landed.at[pieces - 1, :, pl.ds(0, seg_len - rows), pl.ds(0, R)], send_sem.at[pieces - 1])
    edge_copy.wait_send()


def per_device(record, fir_taps, pair_offsets):
    n_chan, n_time = lax.axis_size("chan"), lax.axis_size("tm")
    segs, rows, channels = record.shape
    seg_len, block, pairs = rows * n_chan, channels // n_chan, pair_offsets.shape[0]
    pieces = block // WIDE + 1
    forward, inverse = tables(seg_len, 1.0 / math.sqrt(segs * n_time * seg_len))
    inv_high = inverse.astype(jnp.bfloat16)
    inv_low = (inverse - inv_high.astype(np.float32)).astype(jnp.bfloat16)
    lanes = 2 * seg_len // LANES
    vmem, smem = pl.BlockSpec(memory_space=pltpu.VMEM), pl.BlockSpec(memory_space=pltpu.SMEM)
    anywhere = pl.BlockSpec(memory_space=pl.ANY)
    result, _ = pl.pallas_call(
        functools.partial(kernel, n_chan, n_time),
        out_shape=(
            jax.ShapeDtypeStruct((pairs // n_time, seg_len, block), F32),
            jax.ShapeDtypeStruct((pieces, segs, seg_len, WIDE), F32),
        ),
        in_specs=[anywhere, smem, smem, vmem, vmem, vmem],
        out_specs=(vmem, anywhere),
        scratch_shapes=[
            pltpu.VMEM((segs, lanes, 2 * WIDE, LANES), F32),
            pltpu.VMEM((pairs, WIDE, 2 * seg_len), F32),
            pltpu.VMEM((2, pairs, seg_len, WIDE), F32),
            pltpu.VMEM((pieces - 1, n_time - 1, pairs // n_time, seg_len, WIDE), F32),
            pltpu.VMEM((SLOTS, seg_len, WIDE), F32),
            pltpu.VMEM((seg_len, 2 * seg_len), BF16),
            pltpu.VMEM((seg_len, 2 * seg_len), BF16),
            pltpu.SemaphoreType.DMA((pieces + 1,)),
            pltpu.SemaphoreType.DMA((pieces,)),
            pltpu.SemaphoreType.DMA((SLOTS,)),
            pltpu.SemaphoreType.DMA((2,)),
            pltpu.SemaphoreType.DMA((pieces - 1,)),
        ],
        compiler_params=pltpu.CompilerParams(
            collective_id=0, has_side_effects=True, vmem_limit_bytes=60 * 2**20
        ),
    )(record, fir_taps, pair_offsets, forward, inv_high, inv_low)
    return result


def solution(mesh):
    placed = (P("tm", "chan", None), P(), P())
    return jax.shard_map(
        per_device, mesh=mesh, in_specs=placed, out_specs=P("tm", None, "chan"), check_vma=False
    )
```
